32 devices in a mesh: groups: 2 (over x), row: 16 (over z, y, core).
Axes of the slice: x: 2, y: 2, z: 4, core: 2. Of those that a mesh axis runs over, the one named last changes fastest.
Arguments:
- exterior_map: bfloat16 [15360, 7680], P(('groups', 'row')), parts along dimension 0, may hold values from -6 to 6
- couple_maps: bfloat16 [4, 7680, 1024], P('groups', 'row'), parts along dimension 0, may hold values from -0.1875 to 0.1875
- face_from_exterior: bfloat16 [15360, 1024], P(('groups', 'row')), parts along dimension 0, may hold values from -12 to 12
- face_maps: float32 [4096, 1024], P(('groups', 'row')), parts along dimension 0, may hold values from -1 to 2
- start_inverse: float32 [2048, 1024], P('groups'), parts along dimension 0, may hold values from -1 to 1
Outputs:
- merged_columns: bfloat16 [2, 15360, 7680], P(None, ('groups', 'row')), parts along dimension 1
The draws below stay inside these ranges and needn't reach their ends.
There are 2 independent parts, one for each index of `groups`. The reference program is written for one: setup_inputs(seed, part) draws one part's arguments, and reference() takes and returns one part's arrays. A program takes and returns all parts, laid end to end along the dimension named above; each array names one. Nothing has to cross between parts.
All inputs are finite; a program needn't handle non-finite values.
Results may differ from the reference program's by a relative error of at most 0.0095.
Values may be sent and summed in bfloat16 or wider, within the bound.
A program may use at most 128 MiB of HBM per device.

```python
import math
import jax
import jax.numpy as jnp
from jax import lax

E = 7680
S = 1024
NEWTON = 2


def face_parts(key):
    base = jax.random.fold_in(key, 7001)
    keys = jax.random.split(base, 5)
    diag_first = jax.random.uniform(keys[0], (S,), jnp.float32, 1.0, 1.5)
    diag_second = jax.random.uniform(keys[1], (S,), jnp.float32, 1.0, 1.5)
    noise_first = jnp.clip(jax.random.normal(keys[2], (S, S), jnp.float32), -4.0, 4.0)
    noise_second = jnp.clip(jax.random.normal(keys[3], (S, S), jnp.float32), -4.0, 4.0)
    extra = jnp.clip(jax.random.normal(keys[4], (S, S), jnp.float32), -4.0, 4.0)
    scale_root = 1.0 / math.sqrt(S)
    face_first = jnp.diag(diag_first) + 0.71 * scale_root * noise_first
    face_second = jnp.diag(diag_second) + 0.71 * scale_root * noise_second
    recip = 1.0 / (diag_first + diag_second)
    inverse = jnp.diag(recip) - recip[:, None] * (1.2 * scale_root * extra) * recip[None, :]
    return (face_first, face_second, inverse)


def draw_face_maps(key, part):
    face_first, face_second, inverse = face_parts(key)
    return jnp.concatenate([face_first, face_second], axis=0)


def draw_start_inverse(key, part):
    face_first, face_second, inverse = face_parts(key)
    return inverse


def block_levels(own_key, dims, shards, low, top_value):
    loudness = 1.0
    for dim, blocks in shards:
        draws = jax.random.uniform(jax.random.fold_in(jax.random.fold_in(own_key, 6), dim), (blocks,), jnp.float32, low / len(shards), top_value / len(shards))
        loudness = loudness * jnp.repeat(jnp.exp(draws), dims[dim] // blocks).reshape((-1,) + (1,) * (len(dims) - 1 - dim))
    return loudness


def bell_draw(own_key, shape, width, reach, cuts=(), dtype=jnp.bfloat16):
    array = jax.random.normal(own_key, shape, jnp.float32) * width
    if len(cuts) > 0:
        array = block_levels(own_key, shape, cuts, -0.22, 0.18) * array
    return jnp.clip(array, min=-reach, max=reach).astype(dtype)


def setup_inputs(seed: int = 0, part: int = 0) -> dict:
    streams_of = jax.random.split(jax.random.key(seed), 6)
    part_keys = jax.random.split(jax.random.fold_in(streams_of[5], part), 6)
    exterior_map = bell_draw(part_keys[0], (E, E), 1.0, 6.0, ((0, 16),))
    couple_maps = bell_draw(part_keys[1], (2, E, S), S ** -0.5, 0.1875, ((1, 16),))
    face_from_exterior = bell_draw(part_keys[2], (E, S), 3.0, 12.0, ((0, 16),))
    face_maps = draw_face_maps(jax.random.fold_in(jax.random.fold_in(streams_of[5], part), 71), part)
    start_inverse = draw_start_inverse(jax.random.fold_in(jax.random.fold_in(streams_of[5], part), 71), part)
    return dict(exterior_map=exterior_map, couple_maps=couple_maps, face_from_exterior=face_from_exterior, face_maps=face_maps, start_inverse=start_inverse)


def reference(exterior_map, couple_maps, face_from_exterior, face_maps, start_inverse):
    high = lax.Precision.HIGHEST
    coupling = face_maps[:S] + face_maps[S:]
    iterate = start_inverse
    for newton_step in range(NEWTON):
        product = jnp.dot(coupling, iterate, precision=high, preferred_element_type=jnp.float32)
        iterate = 2.0 * iterate - jnp.dot(iterate, product, precision=high, preferred_element_type=jnp.float32)
    panel_rows = face_from_exterior.astype(jnp.float32)
    face_image = jnp.dot(iterate, panel_rows.T, precision=high, preferred_element_type=jnp.float32).astype(jnp.bfloat16)
    upper = jnp.dot(couple_maps[0], face_image, preferred_element_type=jnp.float32)
    lower = jnp.dot(couple_maps[1], face_image, preferred_element_type=jnp.float32)
    merged_upper = (exterior_map.astype(jnp.float32) - upper).astype(jnp.bfloat16)
    merged_lower = (-lower).astype(jnp.bfloat16)
    return jnp.stack([merged_upper, merged_lower])
```

```python
import jax
import jax.numpy as jnp
from jax import lax
from jax.sharding import PartitionSpec as P


def per_device(exterior_map, couple_maps, face_from_exterior, face_maps, start_inverse):
    high = lax.Precision.HIGHEST
    f32 = jnp.float32
    bf16 = jnp.bfloat16
    devices = lax.axis_size("row")
    position = lax.axis_index("row")
    halfway = devices // 2
    width = start_inverse.shape[0]
    rows = face_maps.shape[0] // 2
    side = position // halfway
    panels = lax.all_gather(face_from_exterior, "row", axis=0, tiled=True)
    mine = lax.dynamic_slice_in_dim(face_maps, side * rows, rows, 0)
    theirs = lax.dynamic_slice_in_dim(face_maps, (1 - side) * rows, rows, 0)
    route = [((i - halfway) % devices, i) for i in range(devices)]
    received = lax.ppermute(theirs.astype(bf16), "row", route).astype(f32)
    coupling = mine + received
    start = 2 * rows * (position % halfway) + rows * side
    product = jnp.dot(coupling, start_inverse, precision=high, preferred_element_type=f32)
    row_index = start + lax.broadcasted_iota(jnp.int32, product.shape, 0)
    col_index = lax.broadcasted_iota(jnp.int32, product.shape, 1)
    residual = (row_index == col_index).astype(f32) - product
    gathered = lax.all_gather(residual.astype(bf16), "row", axis=0, tiled=True)
    residual = gathered.reshape(2, halfway, rows, width).transpose(1, 0, 2, 3).reshape(width, width)
    maps = couple_maps.reshape(-1, width)
    first = jnp.dot(maps.astype(f32), start_inverse, precision=lax.Precision.HIGH, preferred_element_type=f32)
    square = jnp.dot(residual, residual, preferred_element_type=f32).astype(bf16)
    second = first + jnp.dot(first.astype(bf16), residual, preferred_element_type=f32)
    third = second + jnp.dot(second.astype(bf16), square, preferred_element_type=f32)
    left = third.astype(bf16).reshape(couple_maps.shape)
    update = jnp.einsum("bis,es->bie", left, panels, preferred_element_type=f32)
    return jnp.stack([exterior_map.astype(f32) - update[0], -update[1]]).astype(bf16)


def solution(mesh):
    return jax.shard_map(
        per_device,
        mesh=mesh,
        in_specs=(
            P(("groups", "row"), None),
            P("groups", "row", None),
            P(("groups", "row"), None),
            P(("groups", "row"), None),
            P("groups", None),
        ),
        out_specs=P(None, ("groups", "row"), None),
        check_vma=False,
    )
```

```python
import functools

import jax
import jax.numpy as jnp
from jax import lax
from jax.experimental import pallas as pl
from jax.experimental.pallas import tpu as pltpu
from jax.sharding import PartitionSpec as P

F32 = jnp.float32
BF16 = jnp.bfloat16
LANES = 128
RIGHT, LEFT, ACROSS, CORE_OWN, CORE_OTHER = range(5)


def tile_width(span):
    return max(w for w in range(LANES, 641, LANES) if span % w == 0)


def kernel(
    n,
    ext_ref,
    maps_ref,
    panel_ref,
    face_ref,
    start_ref,
    out_ref,
    panels,
    resid,
    ext,
    maps,
    start,
    start_hi,
    start_lo,
    image,
    left,
    square,
    stage,
    face_out,
    face_in,
    local_sem,
    out_sem,
    face_sem,
    send_sem,
    recv_sem,
):
    line = n // 4
    halfway = n // 2
    block = panel_ref.shape[0]
    half = face_ref.shape[0] // 2
    width = start.shape[0]
    me = lax.axis_index("row")
    z, y, c = me // 4, (me // 2) % 2, me % 2
    side = me // halfway
    sibling = (me + halfway) % n
    has_right, has_left = z < line - 1, z > 0

    def device(zz, yy, cc):
        return zz * 4 + yy * 2 + cc

    local = [
        pltpu.make_async_copy(start_ref, start, local_sem.at[0]),
        pltpu.make_async_copy(maps_ref, maps, local_sem.at[1]),
        pltpu.make_async_copy(
            panel_ref,
            panels.at[pl.ds(pl.multiple_of(me * block, 16), block)],
            local_sem.at[2],
        ),
        pltpu.make_async_copy(ext_ref, ext, local_sem.at[3]),
    ]
    for copy in local:
        copy.start()

    barrier = pltpu.get_barrier_semaphore()

    def greet(target):
        pl.semaphore_signal(
            barrier, inc=1, device_id={"row": target}, device_id_type=pl.DeviceIdType.MESH
        )

    greet(device(z, 1 - y, c))
    greet(device(z, y, 1 - c))
    greet(sibling)

    @pl.when(has_right)
    def _():
        greet(me + 4)

    @pl.when(has_left)
    def _():
        greet(me - 4)

    face_out[...] = face_ref[pl.ds(pl.multiple_of((1 - side) * half, 16), half)].astype(BF16)
    pl.semaphore_wait(barrier, 3 + has_right.astype(jnp.int32) + has_left.astype(jnp.int32))

    exchange = pltpu.make_async_remote_copy(
        src_ref=face_out,
        dst_ref=face_in,
        send_sem=face_sem.at[0],
        recv_sem=face_sem.at[1],
        device_id={"row": sibling},
        device_id_type=pl.DeviceIdType.MESH,
    )
    exchange.start()

    def panel_rows(dev):
        return panels.at[pl.ds(pl.multiple_of(dev * block, 16), block)]

    def resid_start(dev):
        return pl.multiple_of((2 * (dev % halfway) + dev // halfway) * half, 16)

    def resid_rows(dev):
        return resid.at[pl.ds(resid_start(dev), half)]

    def copy_of(kind, rows_of, way, dev, source=None):
        target = {
            RIGHT: me + 4,
            LEFT: me - 4,
            ACROSS: device(z, 1 - y, c),
            CORE_OWN: device(z, y, 1 - c),
            CORE_OTHER: device(z, y, 1 - c),
        }[way]
        return pltpu.make_async_remote_copy(
            src_ref=rows_of(dev) if source is None else source,
            dst_ref=rows_of(dev),
            send_sem=send_sem.at[kind, way, dev // 4],
            recv_sem=recv_sem.at[kind, dev],
            device_id={"row": target},
            device_id_type=pl.DeviceIdType.MESH,
        )

    def relay(kind, rows_of):
        def send_own(source):
            copy_of(kind, rows_of, ACROSS, me, source).start()

            @pl.when(has_right)
            def _():
                copy_of(kind, rows_of, RIGHT, me, source).start()

            @pl.when(has_left)
            def _():
                copy_of(kind, rows_of, LEFT, me, source).start()

            copy_of(kind, rows_of, CORE_OWN, me, source).start()

        def wait(dev):
            copy_of(kind, rows_of, CORE_OWN, dev).wait_recv()

        def at_step(step, act):
            if step == 0:
                act(z)
            else:

                @pl.when(z >= step)
                def _():
                    act(z - step)

                @pl.when(z + step < line)
                def _():
                    act(z + step)

        def along(step):
            @pl.when(z >= step)
            def _():
                dev = device(z - step, y, c)
                wait(dev)

                @pl.when(has_right)
                def _():
                    copy_of(kind, rows_of, RIGHT, dev).start()

                copy_of(kind, rows_of, ACROSS, dev).start()
                copy_of(kind, rows_of, CORE_OWN, dev).start()

            @pl.when(z + step < line)
            def _():
                dev = device(z + step, y, c)
                wait(dev)

                @pl.when(has_left)
                def _():
                    copy_of(kind, rows_of, LEFT, dev).start()

                copy_of(kind, rows_of, ACROSS, dev).start()
                copy_of(kind, rows_of, CORE_OWN, dev).start()

        def across(step):
            def act(zz):
                dev = device(zz, 1 - y, c)
                wait(dev)
                copy_of(kind, rows_of, CORE_OTHER, dev).start()

            at_step(step, act)

        def core(step):
            def act(zz):
                wait(device(zz, y, 1 - c))
                wait(device(zz, 1 - y, 1 - c))

            at_step(step, act)

        def finish():
            @pl.loop(0, line)
            def _(zz):
                dev = device(zz, y, c)

                @pl.when(has_right & (zz <= z))
                def _():
                    copy_of(kind, rows_of, RIGHT, dev).wait_send()

                @pl.when(has_left & (zz >= z))
                def _():
                    copy_of(kind, rows_of, LEFT, dev).wait_send()

                copy_of(kind, rows_of, ACROSS, dev).wait_send()
                copy_of(kind, rows_of, CORE_OWN, dev).wait_send()
                copy_of(kind, rows_of, CORE_OTHER, device(zz, 1 - y, c)).wait_send()

        return send_own, along, across, core, finish, at_step

    send_panel, panel_along, panel_across, panel_core, panel_finish, at_step = relay(0, panel_rows)
    send_resid, resid_along, resid_across, resid_core, resid_finish, _ = relay(1, resid_rows)

    send_panel(panel_ref)

    local[0].wait()
    start_hi[...] = start[...].astype(BF16)
    start_lo[...] = (start[...] - start_hi[...].astype(F32)).astype(BF16)
    exchange.wait()
    coupling = face_ref[pl.ds(pl.multiple_of(side * half, 16), half)] + face_in[...].astype(F32)
    coupling_hi = coupling.astype(BF16)
    coupling_lo = (coupling - coupling_hi.astype(F32)).astype(BF16)
    product = jnp.dot(coupling_hi, start_hi[...], preferred_element_type=F32)
    product += jnp.dot(coupling_hi, start_lo[...], preferred_element_type=F32)
    product += jnp.dot(coupling_lo, start_hi[...], preferred_element_type=F32)
    first = resid_start(me)
    row_index = first + lax.broadcasted_iota(jnp.int32, product.shape, 0)
    col_index = lax.broadcasted_iota(jnp.int32, product.shape, 1)
    identity = jnp.where(row_index == col_index, 1.0, 0.0)
    resid[pl.ds(first, half)] = (identity - product).astype(BF16)
    send_resid(resid_rows(me))

    local[1].wait()

    @pl.loop(0, 2)
    def _(box):
        image[box] = jnp.dot(
            maps[box], start_hi[...], preferred_element_type=F32
        ) + jnp.dot(maps[box], start_lo[...], preferred_element_type=F32)

    for step in range(1, line):
        resid_along(step)
    panel_along(1)
    for step in range(line):
        resid_across(step)
    for step in range(line):
        resid_core(step)

    square_rows = width // 4

    @pl.loop(0, 4)
    def _(part):
        rows = pl.ds(pl.multiple_of(part * square_rows, 16), square_rows)
        square[rows] = jnp.dot(resid[rows], resid[...], preferred_element_type=F32).astype(BF16)

    @pl.loop(0, 2)
    def _(box):
        value = image[box]
        value += jnp.dot(value.astype(BF16), resid[...], preferred_element_type=F32)
        value += jnp.dot(value.astype(BF16), square[...], preferred_element_type=F32)
        left[box] = value.astype(BF16)

    local[2].wait()
    local[3].wait()

    def columns(begin, span):
        tile = stage.shape[-1]
        tiles = span // tile

        def copy_out(at, slot):
            at = pl.multiple_of(at, LANES)
            return pltpu.make_async_copy(
                stage.at[slot], out_ref.at[:, :, pl.ds(at, tile)], out_sem.at[slot]
            )

        @pl.loop(0, tiles)
        def _(index):
            slot = index % 2
            at = pl.multiple_of(begin + index * tile, LANES)

            @pl.when(index >= 2)
            def _():
                copy_out(at, slot).wait()

            part = panels[pl.ds(at, tile)]
            contract = (((1,), (1,)), ((), ()))
            upper = lax.dot_general(left[0], part, contract, preferred_element_type=F32)
            stage[slot, 0] = (ext[:, pl.ds(at, tile)].astype(F32) - upper).astype(BF16)
            lower = lax.dot_general(left[1], part, contract, preferred_element_type=F32)
            stage[slot, 1] = (-lower).astype(BF16)
            copy_out(at, slot).start()

        for index in range(max(tiles - 2, 0), tiles):
            copy_out(begin, index % 2).wait()

    group = 4 * block
    aligned = group % LANES == 0
    for step in range(line):
        if step > 0 and step + 1 < line:
            panel_along(step + 1)
        panel_across(step)
        panel_core(step)
        if aligned:
            at_step(step, lambda zz: columns(zz * group, group))
    if not aligned:
        columns(0, panels.shape[0])

    panel_finish()
    resid_finish()


def per_device(n, exterior_map, couple_maps, face_from_exterior, face_maps, start_inverse):
    block, width = face_from_exterior.shape
    half = face_maps.shape[0] // 2
    exterior = n * block
    group = 4 * block
    tile = tile_width(group if group % LANES == 0 else exterior)
    anywhere = pl.BlockSpec(memory_space=pl.ANY)
    in_vmem = pl.BlockSpec(memory_space=pltpu.VMEM)
    out_shape = jax.ShapeDtypeStruct((2, exterior_map.shape[0], exterior), BF16)
    return pl.pallas_call(
        functools.partial(kernel, n),
        out_shape=out_shape,
        in_specs=[anywhere, anywhere, anywhere, in_vmem, anywhere],
        out_specs=anywhere,
        scratch_shapes=[
            pltpu.VMEM((exterior, width), BF16),
            pltpu.VMEM((width, width), BF16),
            pltpu.VMEM(exterior_map.shape, BF16),
            pltpu.VMEM(couple_maps.shape, BF16),
            pltpu.VMEM((width, width), F32),
            pltpu.VMEM((width, width), BF16),
            pltpu.VMEM((width, width), BF16),
            pltpu.VMEM(couple_maps.shape, F32),
            pltpu.VMEM(couple_maps.shape, BF16),
            pltpu.VMEM((width, width), BF16),
            pltpu.VMEM((2, 2, exterior_map.shape[0], tile), BF16),
            pltpu.VMEM((half, width), BF16),
            pltpu.VMEM((half, width), BF16),
            pltpu.SemaphoreType.DMA((4,)),
            pltpu.SemaphoreType.DMA((2,)),
            pltpu.SemaphoreType.DMA((2,)),
            pltpu.SemaphoreType.DMA((2, 5, n // 4)),
            pltpu.SemaphoreType.DMA((2, n)),
        ],
        compiler_params=pltpu.CompilerParams(
            collective_id=0, has_side_effects=True, vmem_limit_bytes=60 * 1024 * 1024
        ),
    )(exterior_map, couple_maps, face_from_exterior, face_maps, start_inverse)


def solution(mesh):
    return jax.shard_map(
        functools.partial(per_device, mesh.shape["row"]),
        mesh=mesh,
        in_specs=(
            P(("groups", "row"), None),
            P("groups", "row", None),
            P(("groups", "row"), None),
            P(("groups", "row"), None),
            P("groups", None),
        ),
        out_specs=P(None, ("groups", "row"), None),
        check_vma=False,
    )
```

```python
import functools

import jax
import jax.numpy as jnp
from jax import lax
from jax.experimental import pallas as pl
from jax.experimental.pallas import tpu as pltpu
from jax.sharding import PartitionSpec as P

F32 = jnp.float32
BF16 = jnp.bfloat16
LANES = 128
CHUNKS = 3
RIGHT, LEFT, RIGHT_OTHER, LEFT_OTHER, ACROSS, CORE_OWN, CORE_OTHER = range(7)


def halves(span):
    first = -(-span // (2 * LANES)) * LANES
    return ((0, first), (first, span - first)) if span > first else ((0, span),)


def kernel(
    n,
    ext_ref,
    maps_ref,
    panel_ref,
    face_ref,
    start_ref,
    out_ref,
    panels,
    resid,
    ext,
    maps,
    start,
    start_hi,
    start_lo,
    image,
    left,
    square,
    stage,
    face_out,
    face_in,
    local_sem,
    out_sem,
    face_sem,
    send_sem,
    recv_sem,
):
    line = n // 4
    halfway = n // 2
    block = panel_ref.shape[0]
    half = face_ref.shape[0] // 2
    width = start.shape[0]
    me = lax.axis_index("row")
    z, y, c = me // 4, (me // 2) % 2, me % 2
    side = me // halfway
    sibling = (me + halfway) % n
    has_right, has_left = z < line - 1, z > 0

    def device(zz, yy, cc):
        return zz * 4 + yy * 2 + cc

    local = [
        pltpu.make_async_copy(start_ref, start, local_sem.at[0]),
        pltpu.make_async_copy(maps_ref, maps, local_sem.at[1]),
        pltpu.make_async_copy(
            panel_ref,
            panels.at[pl.ds(pl.multiple_of(me * block, 16), block)],
            local_sem.at[2],
        ),
        pltpu.make_async_copy(ext_ref, ext, local_sem.at[3]),
    ]
    for copy in local:
        copy.start()

    barrier = pltpu.get_barrier_semaphore()

    def greet(target):
        pl.semaphore_signal(
            barrier, inc=1, device_id={"row": target}, device_id_type=pl.DeviceIdType.MESH
        )

    greet(device(z, 1 - y, c))
    greet(device(z, y, 1 - c))
    greet(sibling)

    @pl.when(has_right)
    def _():
        greet(me + 4)

    @pl.when(has_left)
    def _():
        greet(me - 4)

    face_out[...] = face_ref[pl.ds(pl.multiple_of((1 - side) * half, 16), half)].astype(BF16)
    pl.semaphore_wait(barrier, 3 + has_right.astype(jnp.int32) + has_left.astype(jnp.int32))

    exchange = pltpu.make_async_remote_copy(
        src_ref=face_out,
        dst_ref=face_in,
        send_sem=face_sem.at[0],
        recv_sem=face_sem.at[1],
        device_id={"row": sibling},
        device_id_type=pl.DeviceIdType.MESH,
    )
    exchange.start()

    chunk = block // CHUNKS

    def panel_rows(dev, part):
        return panels.at[pl.ds(pl.multiple_of(dev * block + part * chunk, 16), chunk)]

    def resid_start(dev):
        return pl.multiple_of((2 * (dev % halfway) + dev // halfway) * half, 16)

    def resid_rows(dev, part):
        return resid.at[pl.ds(resid_start(dev), half)]

    rows_of = (panel_rows, resid_rows)

    def copy_of(kind, way, dev, part, source=None):
        target = {
            RIGHT: me + 4,
            LEFT: me - 4,
            RIGHT_OTHER: me + 4,
            LEFT_OTHER: me - 4,
            ACROSS: device(z, 1 - y, c),
            CORE_OWN: device(z, y, 1 - c),
            CORE_OTHER: device(z, y, 1 - c),
        }[way]
        rows = rows_of[kind](dev, part)
        return pltpu.make_async_remote_copy(
            src_ref=rows if source is None else source,
            dst_ref=rows,
            send_sem=send_sem.at[kind, way, dev // 4, part],
            recv_sem=recv_sem.at[kind, dev, part],
            device_id={"row": target},
            device_id_type=pl.DeviceIdType.MESH,
        )

    def await_block(kind, dev, part):
        copy_of(kind, CORE_OWN, dev, part).wait_recv()

    def at_step(step, act):
        if step == 0:
            act(z)
        else:

            @pl.when(z >= step)
            def _():
                act(z - step)

            @pl.when(z + step < line)
            def _():
                act(z + step)

    def send_right(kind, way, dev, part, source=None):
        @pl.when(has_right)
        def _():
            copy_of(kind, way, dev, part, source).start()

    def send_left(kind, way, dev, part, source=None):
        @pl.when(has_left)
        def _():
            copy_of(kind, way, dev, part, source).start()

    def along(step, act):
        @pl.when(z >= step)
        def _():
            act(z - step, send_right, (RIGHT, RIGHT_OTHER))

        @pl.when(z + step < line)
        def _():
            act(z + step, send_left, (LEFT, LEFT_OTHER))

    def panel_send():
        for part in range(CHUNKS):
            source = panel_ref.at[pl.ds(part * chunk, chunk)]
            copy_of(0, ACROSS, me, part, source).start()
            send_right(0, RIGHT, me, part, source)
            send_left(0, LEFT, me, part, source)
            copy_of(0, CORE_OWN, me, part, source).start()

    def panel_along(step, part):
        def act(zz, send, ways):
            dev = device(zz, y, c)
            await_block(0, dev, part)
            send(0, ways[0], dev, part)
            copy_of(0, ACROSS, dev, part).start()
            copy_of(0, CORE_OWN, dev, part).start()

        along(step, act)

    def panel_across(step):
        def act(zz):
            for part in range(CHUNKS):
                dev = device(zz, 1 - y, c)
                await_block(0, dev, part)
                copy_of(0, CORE_OTHER, dev, part).start()

        at_step(step, act)

    def panel_core(step, column):
        def act(zz):
            for part in range(CHUNKS):
                await_block(0, device(zz, column, 1 - c), part)

        at_step(step, act)

    def resid_across():
        dev = device(z, 1 - y, c)
        await_block(1, dev, 0)
        send_right(1, RIGHT_OTHER, dev, 0)
        send_left(1, LEFT_OTHER, dev, 0)
        copy_of(1, CORE_OTHER, dev, 0).start()

    def resid_along(step):
        def act(zz, send, ways):
            dev = device(zz, y, c)
            await_block(1, dev, 0)
            send(1, ways[0], dev, 0)
            copy_of(1, CORE_OWN, dev, 0).start()
            dev = device(zz, 1 - y, c)
            await_block(1, dev, 0)
            send(1, ways[1], dev, 0)
            copy_of(1, CORE_OTHER, dev, 0).start()

        along(step, act)

    def resid_core(step):
        def act(zz):
            await_block(1, device(zz, y, 1 - c), 0)
            await_block(1, device(zz, 1 - y, 1 - c), 0)

        at_step(step, act)

    def finish():
        @pl.loop(0, line)
        def _(zz):
            own, other = device(zz, y, c), device(zz, 1 - y, c)

            @pl.when(has_right & (zz <= z))
            def _():
                for part in range(CHUNKS):
                    copy_of(0, RIGHT, own, part).wait_send()
                copy_of(1, RIGHT, own, 0).wait_send()
                copy_of(1, RIGHT_OTHER, other, 0).wait_send()

            @pl.when(has_left & (zz >= z))
            def _():
                for part in range(CHUNKS):
                    copy_of(0, LEFT, own, part).wait_send()
                copy_of(1, LEFT, own, 0).wait_send()
                copy_of(1, LEFT_OTHER, other, 0).wait_send()

            for part in range(CHUNKS):
                copy_of(0, ACROSS, own, part).wait_send()
                copy_of(0, CORE_OWN, own, part).wait_send()
                copy_of(0, CORE_OTHER, other, part).wait_send()
            copy_of(1, CORE_OWN, own, 0).wait_send()
            copy_of(1, CORE_OTHER, other, 0).wait_send()

        copy_of(1, ACROSS, me, 0).wait_send()

    panel_send()

    local[0].wait()
    local[1].wait()
    start_hi[...] = start[...].astype(BF16)
    start_lo[...] = (start[...] - start_hi[...].astype(F32)).astype(BF16)

    @pl.loop(0, 2)
    def _(box):
        image[box] = jnp.dot(
            maps[box], start_hi[...], preferred_element_type=F32
        ) + jnp.dot(maps[box], start_lo[...], preferred_element_type=F32)

    exchange.wait()
    coupling = face_ref[pl.ds(pl.multiple_of(side * half, 16), half)] + face_in[...].astype(F32)
    coupling_hi = coupling.astype(BF16)
    coupling_lo = (coupling - coupling_hi.astype(F32)).astype(BF16)
    product = jnp.dot(coupling_hi, start_hi[...], preferred_element_type=F32)
    product += jnp.dot(coupling_hi, start_lo[...], preferred_element_type=F32)
    product += jnp.dot(coupling_lo, start_hi[...], preferred_element_type=F32)
    first = resid_start(me)
    row_index = first + lax.broadcasted_iota(jnp.int32, product.shape, 0)
    col_index = lax.broadcasted_iota(jnp.int32, product.shape, 1)
    identity = jnp.where(row_index == col_index, 1.0, 0.0)
    resid[pl.ds(first, half)] = (identity - product).astype(BF16)
    copy_of(1, ACROSS, me, 0).start()
    send_right(1, RIGHT, me, 0)
    send_left(1, LEFT, me, 0)
    copy_of(1, CORE_OWN, me, 0).start()

    panel_along(1, 0)
    panel_along(1, 1)
    resid_across()
    panel_along(1, 2)
    for step in range(1, line):
        resid_along(step)
    for step in range(line):
        resid_core(step)
    if line > 2:
        panel_along(2, 0)

    square_rows = width // 4

    @pl.loop(0, 4)
    def _(part):
        rows = pl.ds(pl.multiple_of(part * square_rows, 16), square_rows)
        square[rows] = jnp.dot(resid[rows], resid[...], preferred_element_type=F32).astype(BF16)

    @pl.loop(0, 2)
    def _(box):
        value = image[box]
        value += jnp.dot(value.astype(BF16), resid[...], preferred_element_type=F32)
        value += jnp.dot(value.astype(BF16), square[...], preferred_element_type=F32)
        left[box] = value.astype(BF16)

    if line > 2:
        panel_along(2, 1)
    local[2].wait()
    local[3].wait()

    def columns(begin, spans):
        copies = []
        for slot, (offset, tile) in enumerate(spans):
            at = pl.multiple_of(begin + offset, LANES)
            part = panels[pl.ds(at, tile)]
            contract = (((1,), (1,)), ((), ()))
            upper = lax.dot_general(left[0], part, contract, preferred_element_type=F32)
            mine = (ext[:, pl.ds(at, tile)].astype(F32) - upper).astype(BF16)
            stage[slot, 0, :, pl.ds(0, tile)] = mine
            lower = lax.dot_general(left[1], part, contract, preferred_element_type=F32)
            stage[slot, 1, :, pl.ds(0, tile)] = (-lower).astype(BF16)
            copies.append(
                pltpu.make_async_copy(
                    stage.at[slot, :, :, pl.ds(0, tile)],
                    out_ref.at[:, :, pl.ds(at, tile)],
                    out_sem.at[slot],
                )
            )
            copies[-1].start()
        for copy in copies:
            copy.wait()

    group = 4 * block
    aligned = group % LANES == 0
    early_width = 2 * block // LANES * LANES
    late_width = group - early_width

    def early(step):
        panel_core(step, y)
        if aligned:
            begin = y * late_width
            at_step(step, lambda zz: columns(zz * group + begin, halves(early_width)))

    def late(step):
        panel_core(step, 1 - y)
        if aligned:
            begin = (1 - y) * early_width
            at_step(step, lambda zz: columns(zz * group + begin, halves(late_width)))

    early(0)
    if line > 2:
        panel_along(2, 2)
    panel_across(0)
    late(0)
    for step in range(1, line):
        early(step)
        if step > 2 and step + 1 < line:
            panel_along(step + 1, 0)
            panel_along(step + 1, 1)
            panel_along(step + 1, 2)
        panel_across(step)
        late(step)
        if step == 1 and line > 3:
            for part in range(CHUNKS):
                panel_along(3, part)
    if not aligned:
        span = 2 * LANES

        @pl.loop(0, panels.shape[0] // span)
        def _(index):
            columns(index * span, ((0, span),))

    finish()


def per_device(n, exterior_map, couple_maps, face_from_exterior, face_maps, start_inverse):
    block, width = face_from_exterior.shape
    half = face_maps.shape[0] // 2
    exterior = n * block
    tile = max(2 * LANES, -(-2 * block // LANES // 2) * LANES)
    anywhere = pl.BlockSpec(memory_space=pl.ANY)
    in_vmem = pl.BlockSpec(memory_space=pltpu.VMEM)
    out_shape = jax.ShapeDtypeStruct((2, exterior_map.shape[0], exterior), BF16)
    return pl.pallas_call(
        functools.partial(kernel, n),
        out_shape=out_shape,
        in_specs=[anywhere, anywhere, anywhere, in_vmem, anywhere],
        out_specs=anywhere,
        scratch_shapes=[
            pltpu.VMEM((exterior, width), BF16),
            pltpu.VMEM((width, width), BF16),
            pltpu.VMEM(exterior_map.shape, BF16),
            pltpu.VMEM(couple_maps.shape, BF16),
            pltpu.VMEM((width, width), F32),
            pltpu.VMEM((width, width), BF16),
            pltpu.VMEM((width, width), BF16),
            pltpu.VMEM(couple_maps.shape, F32),
            pltpu.VMEM(couple_maps.shape, BF16),
            pltpu.VMEM((width, width), BF16),
            pltpu.VMEM((2, 2, exterior_map.shape[0], tile), BF16),
            pltpu.VMEM((half, width), BF16),
            pltpu.VMEM((half, width), BF16),
            pltpu.SemaphoreType.DMA((4,)),
            pltpu.SemaphoreType.DMA((2,)),
            pltpu.SemaphoreType.DMA((2,)),
            pltpu.SemaphoreType.DMA((2, 7, n // 4, CHUNKS)),
            pltpu.SemaphoreType.DMA((2, n, CHUNKS)),
        ],
        compiler_params=pltpu.CompilerParams(
            collective_id=0, has_side_effects=True, vmem_limit_bytes=60 * 1024 * 1024
        ),
    )(exterior_map, couple_maps, face_from_exterior, face_maps, start_inverse)


def solution(mesh):
    return jax.shard_map(
        functools.partial(per_device, mesh.shape["row"]),
        mesh=mesh,
        in_specs=(
            P(("groups", "row"), None),
            P("groups", "row", None),
            P(("groups", "row"), None),
            P(("groups", "row"), None),
            P("groups", None),
        ),
        out_specs=P(None, ("groups", "row"), None),
        check_vma=False,
    )
```

```python
import functools

import jax
import jax.numpy as jnp
from jax import lax
from jax.experimental import pallas as pl
from jax.experimental.pallas import tpu as pltpu
from jax.sharding import PartitionSpec as P

F32 = jnp.float32
BF16 = jnp.bfloat16
LANES = 128
RIGHT, LEFT, ACROSS, CORE_OWN, CORE_OTHER = range(5)


def tile_width(span):
    return max(w for w in range(LANES, 641, LANES) if span % w == 0)


def kernel(
    n,
    ext_ref,
    maps_ref,
    panel_ref,
    face_ref,
    start_ref,
    out_ref,
    panels,
    resid,
    ext,
    maps,
    start,
    start_hi,
    start_lo,
    image,
    left,
    square,
    stage,
    face_out,
    face_in,
    local_sem,
    out_sem,
    face_sem,
    send_sem,
    recv_sem,
):
    line = n // 4
    halfway = n // 2
    block = panel_ref.shape[0]
    half = face_ref.shape[0] // 2
    width = start.shape[0]
    me = lax.axis_index("row")
    z, y, c = me // 4, (me // 2) % 2, me % 2
    side = me // halfway
    sibling = (me + halfway) % n
    has_right, has_left = z < line - 1, z > 0

    def device(zz, yy, cc):
        return zz * 4 + yy * 2 + cc

    local = [
        pltpu.make_async_copy(start_ref, start, local_sem.at[0]),
        pltpu.make_async_copy(maps_ref, maps, local_sem.at[1]),
        pltpu.make_async_copy(
            panel_ref,
            panels.at[pl.ds(pl.multiple_of(me * block, 16), block)],
            local_sem.at[2],
        ),
        pltpu.make_async_copy(ext_ref, ext, local_sem.at[3]),
    ]
    for copy in local:
        copy.start()

    barrier = pltpu.get_barrier_semaphore()

    def greet(target):
        pl.semaphore_signal(
            barrier, inc=1, device_id={"row": target}, device_id_type=pl.DeviceIdType.MESH
        )

    greet(device(z, 1 - y, c))
    greet(device(z, y, 1 - c))
    greet(sibling)

    @pl.when(has_right)
    def _():
        greet(me + 4)

    @pl.when(has_left)
    def _():
        greet(me - 4)

    face_out[...] = face_ref[pl.ds(pl.multiple_of((1 - side) * half, 16), half)].astype(BF16)
    pl.semaphore_wait(barrier, 3 + has_right.astype(jnp.int32) + has_left.astype(jnp.int32))

    exchange = pltpu.make_async_remote_copy(
        src_ref=face_out,
        dst_ref=face_in,
        send_sem=face_sem.at[0],
        recv_sem=face_sem.at[1],
        device_id={"row": sibling},
        device_id_type=pl.DeviceIdType.MESH,
    )
    exchange.start()

    front = block // 32 * 16
    back = block - front

    def front_rows(dev):
        return panels.at[pl.ds(pl.multiple_of(dev * block, 16), front)]

    def back_rows(dev):
        return panels.at[pl.ds(pl.multiple_of(dev * block + front, 16), back)]

    def resid_start(dev):
        return pl.multiple_of((2 * (dev % halfway) + dev // halfway) * half, 16)

    def resid_rows(dev):
        return resid.at[pl.ds(resid_start(dev), half)]

    def copy_of(kind, rows_of, way, dev, source=None):
        target = {
            RIGHT: me + 4,
            LEFT: me - 4,
            ACROSS: device(z, 1 - y, c),
            CORE_OWN: device(z, y, 1 - c),
            CORE_OTHER: device(z, y, 1 - c),
        }[way]
        return pltpu.make_async_remote_copy(
            src_ref=rows_of(dev) if source is None else source,
            dst_ref=rows_of(dev),
            send_sem=send_sem.at[kind, way, dev // 4],
            recv_sem=recv_sem.at[kind, dev],
            device_id={"row": target},
            device_id_type=pl.DeviceIdType.MESH,
        )

    def relay(kind, rows_of):
        def send_own(source):
            copy_of(kind, rows_of, ACROSS, me, source).start()

            @pl.when(has_right)
            def _():
                copy_of(kind, rows_of, RIGHT, me, source).start()

            @pl.when(has_left)
            def _():
                copy_of(kind, rows_of, LEFT, me, source).start()

            copy_of(kind, rows_of, CORE_OWN, me, source).start()

        def wait(dev):
            copy_of(kind, rows_of, CORE_OWN, dev).wait_recv()

        def at_step(step, act):
            if step == 0:
                act(z)
            else:

                @pl.when(z >= step)
                def _():
                    act(z - step)

                @pl.when(z + step < line)
                def _():
                    act(z + step)

        def along(step):
            @pl.when(z >= step)
            def _():
                dev = device(z - step, y, c)
                wait(dev)

                @pl.when(has_right)
                def _():
                    copy_of(kind, rows_of, RIGHT, dev).start()

                copy_of(kind, rows_of, ACROSS, dev).start()
                copy_of(kind, rows_of, CORE_OWN, dev).start()

            @pl.when(z + step < line)
            def _():
                dev = device(z + step, y, c)
                wait(dev)

                @pl.when(has_left)
                def _():
                    copy_of(kind, rows_of, LEFT, dev).start()

                copy_of(kind, rows_of, ACROSS, dev).start()
                copy_of(kind, rows_of, CORE_OWN, dev).start()

        def across(step):
            def act(zz):
                dev = device(zz, 1 - y, c)
                wait(dev)
                copy_of(kind, rows_of, CORE_OTHER, dev).start()

            at_step(step, act)

        def core(step):
            def act(zz):
                wait(device(zz, y, 1 - c))
                wait(device(zz, 1 - y, 1 - c))

            at_step(step, act)

        def finish():
            @pl.loop(0, line)
            def _(zz):
                dev = device(zz, y, c)

                @pl.when(has_right & (zz <= z))
                def _():
                    copy_of(kind, rows_of, RIGHT, dev).wait_send()

                @pl.when(has_left & (zz >= z))
                def _():
                    copy_of(kind, rows_of, LEFT, dev).wait_send()

                copy_of(kind, rows_of, ACROSS, dev).wait_send()
                copy_of(kind, rows_of, CORE_OWN, dev).wait_send()
                copy_of(kind, rows_of, CORE_OTHER, device(zz, 1 - y, c)).wait_send()

        return send_own, along, across, core, finish, at_step

    send_front, front_along, front_across, front_core, front_finish, at_step = relay(0, front_rows)
    send_back, back_along, back_across, back_core, back_finish, _ = relay(2, back_rows)
    send_resid, resid_along, resid_across, resid_core, resid_finish, _ = relay(1, resid_rows)

    send_front(panel_ref.at[pl.ds(0, front)])

    local[0].wait()
    start_hi[...] = start[...].astype(BF16)
    start_lo[...] = (start[...] - start_hi[...].astype(F32)).astype(BF16)
    exchange.wait()
    coupling = face_ref[pl.ds(pl.multiple_of(side * half, 16), half)] + face_in[...].astype(F32)
    coupling_hi = coupling.astype(BF16)
    coupling_lo = (coupling - coupling_hi.astype(F32)).astype(BF16)
    product = jnp.dot(coupling_hi, start_hi[...], preferred_element_type=F32)
    product += jnp.dot(coupling_hi, start_lo[...], preferred_element_type=F32)
    product += jnp.dot(coupling_lo, start_hi[...], preferred_element_type=F32)
    first = resid_start(me)
    row_index = first + lax.broadcasted_iota(jnp.int32, product.shape, 0)
    col_index = lax.broadcasted_iota(jnp.int32, product.shape, 1)
    identity = jnp.where(row_index == col_index, 1.0, 0.0)
    resid[pl.ds(first, half)] = (identity - product).astype(BF16)
    send_resid(resid_rows(me))

    for step in range(1, line):
        resid_along(step)
    send_back(panel_ref.at[pl.ds(front, back)])
    front_along(1)

    local[1].wait()

    @pl.loop(0, 2)
    def _(box):
        image[box] = jnp.dot(
            maps[box], start_hi[...], preferred_element_type=F32
        ) + jnp.dot(maps[box], start_lo[...], preferred_element_type=F32)

    for step in range(line):
        resid_across(step)
    for step in range(line):
        resid_core(step)
    back_along(1)

    square_rows = width // 4

    @pl.loop(0, 4)
    def _(part):
        rows = pl.ds(pl.multiple_of(part * square_rows, 16), square_rows)
        square[rows] = jnp.dot(resid[rows], resid[...], preferred_element_type=F32).astype(BF16)

    @pl.loop(0, 2)
    def _(box):
        value = image[box]
        value += jnp.dot(value.astype(BF16), resid[...], preferred_element_type=F32)
        value += jnp.dot(value.astype(BF16), square[...], preferred_element_type=F32)
        left[box] = value.astype(BF16)

    if line > 2:
        front_along(2)
    local[2].wait()
    local[3].wait()

    def columns(begin, span):
        tile = stage.shape[-1]
        tiles = span // tile

        def copy_out(at, slot):
            at = pl.multiple_of(at, LANES)
            return pltpu.make_async_copy(
                stage.at[slot], out_ref.at[:, :, pl.ds(at, tile)], out_sem.at[slot]
            )

        @pl.loop(0, tiles)
        def _(index):
            slot = index % 2
            at = pl.multiple_of(begin + index * tile, LANES)

            @pl.when(index >= 2)
            def _():
                copy_out(at, slot).wait()

            part = panels[pl.ds(at, tile)]
            contract = (((1,), (1,)), ((), ()))
            upper = lax.dot_general(left[0], part, contract, preferred_element_type=F32)
            stage[slot, 0] = (ext[:, pl.ds(at, tile)].astype(F32) - upper).astype(BF16)
            lower = lax.dot_general(left[1], part, contract, preferred_element_type=F32)
            stage[slot, 1] = (-lower).astype(BF16)
            copy_out(at, slot).start()

        for index in range(max(tiles - 2, 0), tiles):
            copy_out(begin, index % 2).wait()

    group = 4 * block
    aligned = group % LANES == 0
    for step in range(line):
        if step > 0 and step + 1 < line:
            if step > 1:
                front_along(step + 1)
            back_along(step + 1)
        front_across(step)
        back_across(step)
        front_core(step)
        back_core(step)
        if aligned:
            at_step(step, lambda zz: columns(zz * group, group))
    if not aligned:
        columns(0, panels.shape[0])

    front_finish()
    back_finish()
    resid_finish()


def per_device(n, exterior_map, couple_maps, face_from_exterior, face_maps, start_inverse):
    block, width = face_from_exterior.shape
    half = face_maps.shape[0] // 2
    exterior = n * block
    group = 4 * block
    tile = tile_width(group if group % LANES == 0 else exterior)
    anywhere = pl.BlockSpec(memory_space=pl.ANY)
    in_vmem = pl.BlockSpec(memory_space=pltpu.VMEM)
    out_shape = jax.ShapeDtypeStruct((2, exterior_map.shape[0], exterior), BF16)
    return pl.pallas_call(
        functools.partial(kernel, n),
        out_shape=out_shape,
        in_specs=[anywhere, anywhere, anywhere, in_vmem, anywhere],
        out_specs=anywhere,
        scratch_shapes=[
            pltpu.VMEM((exterior, width), BF16),
            pltpu.VMEM((width, width), BF16),
            pltpu.VMEM(exterior_map.shape, BF16),
            pltpu.VMEM(couple_maps.shape, BF16),
            pltpu.VMEM((width, width), F32),
            pltpu.VMEM((width, width), BF16),
            pltpu.VMEM((width, width), BF16),
            pltpu.VMEM(couple_maps.shape, F32),
            pltpu.VMEM(couple_maps.shape, BF16),
            pltpu.VMEM((width, width), BF16),
            pltpu.VMEM((2, 2, exterior_map.shape[0], tile), BF16),
            pltpu.VMEM((half, width), BF16),
            pltpu.VMEM((half, width), BF16),
            pltpu.SemaphoreType.DMA((4,)),
            pltpu.SemaphoreType.DMA((2,)),
            pltpu.SemaphoreType.DMA((2,)),
            pltpu.SemaphoreType.DMA((3, 5, n // 4)),
            pltpu.SemaphoreType.DMA((3, n)),
        ],
        compiler_params=pltpu.CompilerParams(
            collective_id=0, has_side_effects=True, vmem_limit_bytes=60 * 1024 * 1024
        ),
    )(exterior_map, couple_maps, face_from_exterior, face_maps, start_inverse)


def solution(mesh):
    return jax.shard_map(
        functools.partial(per_device, mesh.shape["row"]),
        mesh=mesh,
        in_specs=(
            P(("groups", "row"), None),
            P("groups", "row", None),
            P(("groups", "row"), None),
            P(("groups", "row"), None),
            P("groups", None),
        ),
        out_specs=P(None, ("groups", "row"), None),
        check_vma=False,
    )
```
